512 devices in a mesh: inner: 16 (over z_hi, y, core), outer: 32 (over x, z_lo).
Axes of the slice: x: 4, y: 4, z: 16 (z_hi: 2, z_lo: 8; z = z_hi * 8 + z_lo), core: 2. Of those that a mesh axis runs over, the one named last changes fastest.
Arguments:
- queries: bfloat16 [131072, 4096], P(('inner', 'outer')), may hold values from -128 to 128
- keys: bfloat16 [131072, 512], P(('inner', 'outer')), may hold values from -6 to 6
- values: bfloat16 [131072, 512], P(('inner', 'outer')), may hold values from -6 to 6
- spans: int32 [512, 2], replicated, may hold values from 0 to 1023, as said below
Outputs:
- attended: bfloat16 [131072, 4096], P(('inner', 'outer'))
- log_sum: float32 [32, 131072], P(None, ('inner', 'outer'))
The draws below stay inside these ranges and needn't reach their ends.
Inputs may be any that keep to these rules, and one draw needn't show every extreme that they name: `spans`: row d is c and 1023 - c, and every c of 0 to 511 appears in exactly one row.
All inputs are finite; a program needn't handle non-finite values.
Results may differ from the reference program's by a relative error of at most 0.0038.
Values may be sent and summed in bfloat16 or wider, within the bound.
No kernel may reach another device: no remote copies, remote signals or barrier semaphores. Data moves between devices by JAX's collectives and lax.ppermute only.
A program may use at most 128 MiB of HBM per device.

```python
import jax
import jax.numpy as jnp
from jax import lax

TOK_DEV = 256
HQ = 32
KEY_VALUE_HEADS = 4
HEAD_SIZE = 128
QUERY_GROUP_SIZE = 8
SEQUENCE_TOKENS = 131072
N_INNER = 16
N_OUTER = 32
DEVICES = 512


def draw_queries(key, part):
    key = jax.random.fold_in(key, 1)
    array_shape = (SEQUENCE_TOKENS, KEY_VALUE_HEADS, QUERY_GROUP_SIZE, HEAD_SIZE)
    drawn_result = jax.random.truncated_normal(jax.random.fold_in(key, 3), -6.0, 6.0, array_shape, jnp.float32)
    return drawn_result.reshape(SEQUENCE_TOKENS, HQ * HEAD_SIZE).astype(jnp.bfloat16)


def draw_keys(key, part):
    key = jax.random.fold_in(key, 2)
    array_shape = (SEQUENCE_TOKENS, KEY_VALUE_HEADS, HEAD_SIZE)
    drawn_result = jax.random.truncated_normal(jax.random.fold_in(key, 3), -6.0, 6.0, array_shape, jnp.float32)
    return drawn_result.reshape(SEQUENCE_TOKENS, KEY_VALUE_HEADS * HEAD_SIZE).astype(jnp.bfloat16)


def draw_spans(key, part):
    key = jax.random.fold_in(key, 3)
    order = jax.random.permutation(key, DEVICES).astype(jnp.int32)
    return jnp.stack([order, 2 * DEVICES - 1 - order], axis=1).astype(jnp.int32)


def level_of(rng, dims, pieces, least, top_value):
    level, own = 1.0, jax.random.fold_in(rng, 6)
    for position, parts in pieces:
        heights = jnp.exp(jax.random.uniform(jax.random.fold_in(own, position), (parts,), jnp.float32, least / len(pieces), top_value / len(pieces)))
        level = level * jnp.repeat(heights, dims[position] // parts).reshape([-1 if axis == position else 1 for axis in range(len(dims))])
    return level


def noise(rng, dims, spread, most, pieces=(), held_as=jnp.bfloat16):
    array = spread * jax.random.normal(rng, dims, jnp.float32)
    if pieces:
        array = array * level_of(rng, dims, pieces, -0.22, 0.18)
    return jnp.clip(array, -most, most).astype(held_as)


def setup_inputs(seed: int = 0) -> dict:
    splits = jax.random.split(jax.random.key(seed), 5)
    queries = draw_queries(jax.random.fold_in(splits[4], 71), 0)
    keys = draw_keys(jax.random.fold_in(splits[4], 71), 0)
    values = noise(splits[2], (SEQUENCE_TOKENS, KEY_VALUE_HEADS * HEAD_SIZE), 1.0, 6.0, ((0, 512),))
    spans = draw_spans(jax.random.fold_in(splits[4], 71), 0)
    return {"queries": queries, "keys": keys, "values": values, "spans": spans}


def block_positions(pair, row_total):
    offsets = jnp.arange(row_total, dtype=jnp.int32)
    half_rows = row_total // 2
    first = jnp.where(offsets < half_rows, pair[0], pair[1])
    return first * half_rows + offsets % half_rows


def reference(queries, keys, values, spans):
    item_count = N_INNER * N_OUTER
    row_total = TOK_DEV
    key_block_list = keys.reshape(item_count, row_total, KEY_VALUE_HEADS * HEAD_SIZE)
    value_block_list = values.reshape(item_count, row_total, KEY_VALUE_HEADS * HEAD_SIZE)
    query_block_list = queries.reshape(item_count, row_total, HQ * HEAD_SIZE)
    scale = HEAD_SIZE ** -0.5

    def one_device(device_index):
        inner_at = device_index // N_OUTER
        outer_at = device_index % N_OUTER
        source_devices = jnp.stack([device_index, ((inner_at - 1) % N_INNER) * N_OUTER + outer_at,
                             ((inner_at - 2) % N_INNER) * N_OUTER + outer_at,
                             inner_at * N_OUTER + (outer_at - 1) % N_OUTER]).astype(jnp.int32)
        windowed_keys = key_block_list[source_devices].reshape(4 * row_total, KEY_VALUE_HEADS, HEAD_SIZE).astype(jnp.float32)
        windowed_values = value_block_list[source_devices].reshape(4 * row_total, KEY_VALUE_HEADS, HEAD_SIZE).astype(jnp.float32)
        window_pos = jnp.concatenate([block_positions(spans[source_devices[s]], row_total) for s in range(4)])
        query_pos = block_positions(spans[device_index], row_total)
        live = window_pos[None, :] <= query_pos[:, None]
        local_queries = query_block_list[device_index].reshape(row_total, KEY_VALUE_HEADS, QUERY_GROUP_SIZE, HEAD_SIZE).astype(jnp.float32)
        scores = jnp.einsum("rhgd,khd->hgrk", local_queries, windowed_keys) * scale
        scores = jnp.where(live[None, None], scores, -jnp.inf)
        top = jnp.max(scores, axis=-1)
        expo = jnp.exp(scores - top[..., None])
        total = jnp.sum(expo, axis=-1)
        weights = expo.astype(jnp.bfloat16).astype(jnp.float32)
        summed = jnp.einsum("hgrk,khd->rhgd", weights, windowed_values)
        result = summed / jnp.transpose(total, (2, 0, 1))[..., None]
        log_total = (top + jnp.log(total)).reshape(HQ, row_total)
        return result.reshape(row_total, HQ * HEAD_SIZE).astype(jnp.bfloat16), log_total

    outs, logs = lax.map(one_device, jnp.arange(item_count, dtype=jnp.int32))
    attended = outs.reshape(item_count * row_total, HQ * HEAD_SIZE)
    log_sum = jnp.transpose(logs, (1, 0, 2)).reshape(HQ, item_count * row_total)
    return attended, log_sum
```

```python
import functools
import math

import jax
import jax.numpy as jnp
from jax import lax
from jax.experimental import pallas as pl
from jax.experimental.pallas import tpu as pltpu
from jax.sharding import PartitionSpec as P

D = 128
T = 128
GROUP = 8
CHUNK = 4
LOG2E = math.log2(math.e)
SCALE = D**-0.5 * LOG2E
AXES = ("inner", "outer")
Y = 4
CORES = 2


def attend(q, k_ref, v_ref, first, n, masks):
    scores = lax.dot_general(
        q, k_ref[first * T : (first + n) * T, :], (((1,), (1,)), ((), ())), preferred_element_type=jnp.float32
    )
    parts = [scores[:, i * T : (i + 1) * T] for i in range(n)]
    for i, mask in masks.items():
        parts[i] = jnp.where(mask, parts[i], -jnp.inf)
    top = jnp.max(functools.reduce(jnp.maximum, parts), axis=1, keepdims=True) * SCALE
    weights = jnp.concatenate([jnp.exp2(x * SCALE - top).astype(jnp.bfloat16) for x in parts], axis=1)
    summed = lax.dot_general(
        weights, v_ref[first * T : (first + n) * T, :], (((1,), (0,)), ((), ())), preferred_element_type=jnp.float32
    )
    return summed[:, :D], summed[:, D:], top


def attention_body(
    half, meta, spans, q_ref, k_ref, v_ref, near_a, near_b, far_a, far_b, far_c, side_ref, *rest
):
    out_ref, log_ref, k_all, v_all, tops, totals = rest[-6:]
    kv = pl.program_id(0)

    def place(i):
        a = spans[meta[i]]
        flip = a >= 512
        low = pl.multiple_of(jnp.where(flip, T, 0), T)
        high = pl.multiple_of(jnp.where(flip, 0, T), T)
        return jnp.where(flip, 1023 - a, a), low, high

    at_start, at_even = meta[4] == 1, meta[5] == 1
    own, low_at, high_at = place(0)
    blocks = [place(i) for i in range(1, 4)]
    lows = [b[0] < own for b in blocks]
    n_low = sum(x.astype(jnp.int32) for x in lows)
    k_cols = pl.ds(pl.multiple_of(kv * D, D), D)
    v_cols = pl.ds(pl.multiple_of((2 + kv) * D, D), D)
    ones = jnp.ones((T, D), jnp.bfloat16)
    none = jnp.zeros((T, D), jnp.bfloat16)

    def put(slot, k, v, one):
        rows = pl.ds(pl.multiple_of(slot * T, T), T)
        k_all[rows, :] = k
        v_all[rows, :D] = v
        v_all[rows, D:] = one

    def near(rows, cols):
        return jnp.where(at_start & at_even, near_b[rows, cols], near_a[rows, cols])

    def far(rows, cols):
        crossed = far_b[rows, cols] if far_c is None else jnp.where(at_even, far_b[rows, cols], far_c[rows, cols])
        return jnp.where(at_start, crossed, far_a[rows, cols])

    def side(rows, cols):
        return side_ref[rows, cols]

    low_rows, high_rows = pl.ds(low_at, T), pl.ds(high_at, T)
    put(0, k_ref[low_rows, :], v_ref[low_rows, :], ones)
    put(4, k_ref[high_rows, :], v_ref[high_rows, :], ones)
    put(5, k_ref[low_rows, :], v_ref[low_rows, :], ones)
    rank = jnp.int32(0)
    for i, read in enumerate((near, far, side)):
        _, block_low, block_high = blocks[i]
        rows = pl.ds(block_low, T)
        put(6 + i, read(rows, k_cols), read(rows, v_cols), ones)
        rows = pl.ds(pl.multiple_of(jnp.where(lows[i], block_low, block_high), T), T)
        put(jnp.where(lows[i], 1 + rank, 9 + i - rank), read(rows, k_cols), read(rows, v_cols), ones)
        rank = rank + lows[i].astype(jnp.int32)
    many = n_low >= 2
    spare = jnp.where(many, jnp.where(n_low == 2, 3, 9), jnp.where(n_low == 0, 1, 11))
    put(spare, jnp.where(n_low == 2, k_all[T : 2 * T, :], k_ref[low_rows, :]), none, none)

    row = lax.broadcasted_iota(jnp.int32, (CHUNK * T, T), 0) % T
    col = lax.broadcasted_iota(jnp.int32, (CHUNK * T, T), 1)
    lane = lax.broadcasted_iota(jnp.int32, (T, T), 1)

    def chunk_of_heads(g, low_tiles):
        cols = [pl.ds(pl.multiple_of((g * CHUNK + j) * D, D), D) for j in range(CHUNK)]

        def queries(rows):
            return jnp.concatenate([q_ref[rows, c] for c in cols], axis=0)

        masks = {0: col <= row}
        if low_tiles == 2:
            low_masks = {0: col <= row, 1: col <= jnp.where(n_low == 0, row, T)}
        else:
            low_masks = masks
        results = (
            attend(queries(low_rows), k_all, v_all, 0, low_tiles, low_masks),
            attend(queries(high_rows), k_all, v_all, 4, 10 - low_tiles, masks),
        )
        for w, (rows, (summed, total, top)) in enumerate(zip((low_rows, high_rows), results)):
            result = (summed / total).astype(out_ref.dtype)
            for j in range(CHUNK):
                part = slice(j * T, (j + 1) * T)
                out_ref[rows, cols[j]] = result[part]
                here = lane == kv * GROUP + g * CHUNK + j
                tops[w] = jnp.where(here, top[part], tops[w])
                totals[w] = jnp.where(here, total[part], totals[w])

    for low_tiles in (2, 4):

        @pl.when(many == (low_tiles == 4))
        def _():
            def step(g, carry):
                chunk_of_heads(g, low_tiles)
                return carry

            lax.fori_loop(0, GROUP // CHUNK, step, 0, unroll=True)

    @pl.when(kv == 1)
    def _():
        for w, at in enumerate((low_at, high_at)):
            log_sum = (tops[w] + jnp.log2(totals[w])) * (1.0 / LOG2E)
            log_ref[:, pl.ds(at, T)] = jnp.transpose(log_sum)[: 2 * GROUP]


def attention(half, meta, spans, q, k, v, near, far, side, filled=None):
    rows = q.shape[0]
    piece = (rows, 4 * D)

    def heads(i):
        return (0, 2 * half + i)

    def block(array):
        at = half if array.shape[0] > rows else 0
        return pl.BlockSpec(piece, lambda i: (at, 0))

    smem = pl.BlockSpec(memory_space=pltpu.SMEM)
    arrays = [*near, *far, side]
    in_specs = [
        smem,
        smem,
        pl.BlockSpec((rows, GROUP * D), heads),
        pl.BlockSpec((rows, D), heads),
        pl.BlockSpec((rows, D), heads),
    ] + [block(a) for a in arrays]
    args = [meta, spans, q, k, v, *arrays]
    alias = {}
    if filled is not None:
        alias = {len(args): 0, len(args) + 1: 1}
        in_specs += [pl.BlockSpec(memory_space=pl.ANY)] * 2
        args += filled

    def body(*refs):
        refs = list(refs)
        if len(far) == 2:
            refs.insert(9, None)
        attention_body(half, *refs)

    q_heads = q.shape[1] // D
    return pl.pallas_call(
        body,
        grid=(2,),
        out_shape=(
            jax.ShapeDtypeStruct(q.shape, jnp.bfloat16),
            jax.ShapeDtypeStruct((q_heads, rows), jnp.float32),
        ),
        in_specs=in_specs,
        out_specs=(
            pl.BlockSpec((rows, GROUP * D), heads),
            pl.BlockSpec((2 * GROUP, rows), lambda i: (half, 0)),
        ),
        scratch_shapes=[
            pltpu.VMEM((12 * T, D), jnp.bfloat16),
            pltpu.VMEM((12 * T, 2 * D), jnp.bfloat16),
            pltpu.VMEM((2, T, T), jnp.float32),
            pltpu.VMEM((2, T, T), jnp.float32),
        ],
        input_output_aliases=alias,
        compiler_params=pltpu.CompilerParams(vmem_limit_bytes=40 * 2**20),
        cost_estimate=pl.CostEstimate(flops=2_400_000_000, bytes_accessed=4_000_000, transcendentals=2_400_000),
        name=f"attention_{half}",
    )(*args)


def local(n_inner, n_outer, queries, keys, values, spans):
    n_high = n_inner // (Y * CORES)

    def at(high, y, core, o):
        return ((high % n_high * Y + y % Y) * CORES + core) * n_outer + o % n_outer

    def send(block, *moves):
        route = []
        for move in moves:
            for high in range(n_high):
                for o in range(n_outer):
                    for source, target in move(high):
                        route.append((at(*source, o), at(*target, o)))
        return lax.ppermute(block, AXES, sorted(route))

    inner_at = lax.axis_index("inner")
    outer_at = lax.axis_index("outer")
    y_at = inner_at // CORES % Y
    core_at = inner_at % CORES
    meta = jnp.stack(
        [
            inner_at * n_outer + outer_at,
            (inner_at - 1) % n_inner * n_outer + outer_at,
            (inner_at - 2) % n_inner * n_outer + outer_at,
            inner_at * n_outer + (outer_at - 1) % n_outer,
            (y_at == 0).astype(jnp.int32),
            (core_at == 0).astype(jnp.int32),
        ]
    ).astype(jnp.int32)
    first_spans = spans[:, 0]

    width = 2 * D
    first = jnp.concatenate([keys[:, :width], values[:, :width]], axis=1)
    second = jnp.concatenate([keys[:, width:], values[:, width:]], axis=1)
    whole = jnp.concatenate([first, second], axis=0)

    last = Y - 1
    spread_first = send(first, lambda h: [((h, last, 0), (h, 0, 0)), ((h, last, 1), (h, 1, 1))])
    spread_second = send(second, lambda h: [((h, last, 0), (h + 1, 0, 0)), ((h, last, 1), (h, 2, 1))])
    stepped = send(whole, lambda h: [((h, y, c), (h, y + 1, c)) for y in range(last) for c in range(CORES)])
    side = lax.ppermute(
        whole,
        AXES,
        [(i * n_outer + (o - 1) % n_outer, i * n_outer + o) for i in range(n_inner) for o in range(n_outer)],
    )
    crossed_first = send(spread_first, lambda h: [((h, 0, 0), (h + 1, 0, 0)), ((h, 1, 1), (h + 1, 0, 1))])
    crossed_second = send(spread_second, lambda h: [((h, 2, 1), (h + 1, 0, 1))])
    swapped = send(
        jnp.where(core_at == 0, whole, stepped),
        lambda h: [((h, y, 0), (h, y, 1)) for y in range(Y)] + [((h, y, 1), (h, y, 0)) for y in range(1, Y)],
    )
    handed_first = send(crossed_first, lambda h: [((h, 0, 1), (h, 0, 0))])
    handed_second = send(crossed_second, lambda h: [((h, 0, 1), (h, 0, 0))])

    filled = attention(
        0, meta, first_spans, queries, keys, values, (swapped, handed_first), (stepped, crossed_first), side
    )
    return attention(
        1,
        meta,
        first_spans,
        queries,
        keys,
        values,
        (swapped, handed_second),
        (stepped, spread_second, crossed_second),
        side,
        filled,
    )


def solution(mesh):
    placed = P(AXES, None)
    return jax.shard_map(
        functools.partial(local, mesh.shape["inner"], mesh.shape["outer"]),
        mesh=mesh,
        in_specs=(placed, placed, placed, P()),
        out_specs=(placed, P(None, AXES)),
        check_vma=False,
    )
```

```python
import functools
import math

import jax
import jax.numpy as jnp
from jax import lax
from jax.experimental import pallas as pl
from jax.experimental.pallas import tpu as pltpu
from jax.sharding import PartitionSpec as P

D = 128
T = 128
GROUP = 8
CHUNK = 4
LOG2E = math.log2(math.e)
SCALE = D**-0.5 * LOG2E
AXES = ("inner", "outer")
Y = 4
CORES = 2
JOIN = 20_000_000_000


def scores_of(q, k_ref, first, n):
    keys = k_ref[first * T : (first + n) * T, :]
    return lax.dot_general(q, keys, (((1,), (1,)), ((), ())), preferred_element_type=jnp.float32)


def weigh(scores, v_ref, first, n, masks):
    parts = [scores[:, i * T : (i + 1) * T] for i in range(n)]
    for i, mask in masks.items():
        parts[i] = jnp.where(mask, parts[i], -jnp.inf)
    top = jnp.max(functools.reduce(jnp.maximum, parts), axis=1, keepdims=True) * SCALE
    weights = jnp.concatenate([jnp.exp2(x * SCALE - top).astype(jnp.bfloat16) for x in parts], axis=1)
    values = v_ref[first * T : (first + n) * T, :]
    summed = lax.dot_general(weights, values, (((1,), (0,)), ((), ())), preferred_element_type=jnp.float32)
    return top, summed[:, :D], summed[:, D:]


def attention_body(
    meta, spans, q_ref, k_ref, v_ref, handed_k, handed_v, last_k, last_v,
    far_k, far_v, side_k, side_v, out_ref, log_ref, k_all, v_all,
):
    def place(i):
        a = spans[meta[i]]
        flip = a >= 512
        return jnp.where(flip, 1023 - a, a), jnp.where(flip, T, 0), jnp.where(flip, 0, T)

    def rows_at(start):
        return pl.ds(pl.multiple_of(start, T), T)

    at_even = meta[4] == 1

    def near(rows):
        return (
            jnp.where(at_even, last_k[rows, :], handed_k[rows, :]),
            jnp.where(at_even, last_v[rows, :], handed_v[rows, :]),
        )

    def far(rows):
        return far_k[rows, :], far_v[rows, :]

    def side(rows):
        return side_k[rows, :], side_v[rows, :]

    ones = jnp.ones((T, D), v_all.dtype)

    def put(slot, pair, weight=ones):
        rows = rows_at(slot * T)
        k_all[rows, :], v_all[rows, :D] = pair
        v_all[rows, D:] = weight

    own, low_at, high_at = place(0)
    ends = (rows_at(low_at), rows_at(high_at))
    own_low = (k_ref[ends[0], :], v_ref[ends[0], :])
    put(0, own_low)
    put(4, (k_ref[ends[1], :], v_ref[ends[1], :]))
    put(5, own_low)
    n_low = jnp.int32(0)
    for i, read in enumerate((near, far, side)):
        block, block_low, block_high = place(i + 1)
        below = block < own
        put(6 + i, read(rows_at(block_low)))
        put(jnp.where(below, 1 + n_low, 9 + i - n_low), read(rows_at(jnp.where(below, block_low, block_high))))
        n_low = n_low + below.astype(jnp.int32)
    many = n_low >= 2
    spare = jnp.where(many, jnp.where(n_low == 2, 3, 9), jnp.where(n_low == 0, 1, 11))
    none = jnp.zeros((T, D), v_all.dtype)
    put(spare, (jnp.where(n_low == 2, k_all[T : 2 * T, :], own_low[0]), none), none)

    row = lax.broadcasted_iota(jnp.int32, (CHUNK * T, T), 0) % T
    col = lax.broadcasted_iota(jnp.int32, (CHUNK * T, T), 1)
    lane = lax.broadcasted_iota(jnp.int32, (T, T), 1)
    cols = [slice(j * D, (j + 1) * D) for j in range(GROUP)]

    def all_heads(low_tiles):
        first, tiles = (0, 4), (low_tiles, 10 - low_tiles)
        masks = [{0: col <= row}, {0: col <= row}]
        if low_tiles == 2:
            masks[0][1] = col <= jnp.where(n_low == 0, row, T)
        tops, totals = [None, None], [None, None]

        def finish(w, g, scores):
            top, summed, total = weigh(scores, v_all, first[w], tiles[w], masks[w])
            result = (summed * pl.reciprocal(total)).astype(out_ref.dtype)
            for j in range(CHUNK):
                part = slice(j * T, (j + 1) * T)
                out_ref[ends[w], cols[g + j]] = result[part]
                for kept, new in ((tops, top[part]), (totals, total[part])):
                    new = jnp.broadcast_to(new, (T, T))
                    kept[w] = new if kept[w] is None else jnp.where(lane == g + j, new, kept[w])

        waiting = None
        for g in range(0, GROUP, CHUNK):
            for w in (0, 1):
                q = jnp.concatenate([q_ref[ends[w], cols[g + j]] for j in range(CHUNK)], axis=0)
                scores = scores_of(q, k_all, first[w], tiles[w])
                if waiting:
                    finish(*waiting)
                waiting = (w, g, scores)
        finish(*waiting)
        for w in (0, 1):
            log_sum = (tops[w] + jnp.log2(totals[w])) * (1.0 / LOG2E)
            log_ref[:, ends[w]] = jnp.transpose(log_sum)[:GROUP]

    for low_tiles in (2, 4):
        pl.when(many == (low_tiles == 4))(functools.partial(all_heads, low_tiles))


def small_kernel(body, name, flops, outs, *arrays):
    smem = pl.BlockSpec(memory_space=pltpu.SMEM)
    return pl.pallas_call(
        body,
        out_shape=[jax.ShapeDtypeStruct(shape, arrays[-1].dtype) for shape in outs],
        in_specs=[smem if a.ndim == 1 else pl.BlockSpec(a.shape, lambda: (0, 0)) for a in arrays],
        out_specs=[pl.BlockSpec(shape, lambda: (0, 0)) for shape in outs],
        compiler_params=pltpu.CompilerParams(vmem_limit_bytes=16 * 2**20),
        cost_estimate=pl.CostEstimate(flops=flops, bytes_accessed=1_000_000, transcendentals=0),
        name=name,
    )(*arrays)


def pack_body(values, keys, both, relayed, straight, sems):
    rows, cut = values.shape[0], relayed.shape[0]
    copies = [
        (values, relayed.at[:rows]),
        (keys.at[: cut - rows], relayed.at[rows:]),
        (keys.at[cut - rows :], straight),
        (values, both.at[:rows]),
        (keys, both.at[rows:]),
    ]
    copies = [pltpu.make_async_copy(source, to, sems.at[i]) for i, (source, to) in enumerate(copies)]
    for copy in copies:
        copy.start()
    for copy in copies:
        copy.wait()


def pack(values, keys, cut):
    rows, width = keys.shape
    return pl.pallas_call(
        pack_body,
        out_shape=[jax.ShapeDtypeStruct((n, width), keys.dtype) for n in (2 * rows, cut, 2 * rows - cut)],
        in_specs=[pl.BlockSpec(memory_space=pl.ANY)] * 2,
        out_specs=[pl.BlockSpec(memory_space=pltpu.VMEM)] * 3,
        scratch_shapes=[pltpu.SemaphoreType.DMA((5,))],
        compiler_params=pltpu.CompilerParams(vmem_limit_bytes=56 * 2**20),
        name="pack",
    )(values, keys)


def join_body(upper, lower, out):
    rows = upper.shape[0]
    out[:rows, :] = upper[...]
    out[rows:, :] = lower[...]


def choose_body(meta, first, second, out):
    @pl.when(meta[5] == 1)
    def _():
        out[...] = first[...]

    @pl.when(meta[5] == 0)
    def _():
        out[...] = second[...]


def attention(meta, spans, q, *blocks):
    rows, width = q.shape
    smem = pl.BlockSpec(memory_space=pltpu.SMEM)
    vmem = pl.BlockSpec(memory_space=pltpu.VMEM)
    arrays = list({id(array): array for array, _ in blocks}.values())
    where = [([id(a) for a in arrays].index(id(array)), at) for array, at in blocks]

    def body(meta_ref, spans_ref, q_ref, *refs):
        kv = pl.program_id(0)
        columns = pl.ds(pl.multiple_of(kv * D, D), D)
        views = [refs[i].at[at * rows : (at + 1) * rows, columns] for i, at in where]
        q_view = q_ref.at[:, pl.ds(pl.multiple_of(kv * GROUP * D, D), GROUP * D)]
        attention_body(meta_ref, spans_ref, q_view, *views, *refs[len(arrays) :])

    return pl.pallas_call(
        body,
        grid=(width // (GROUP * D),),
        out_shape=(
            jax.ShapeDtypeStruct((rows, width), jnp.bfloat16),
            jax.ShapeDtypeStruct((width // D, rows), jnp.float32),
        ),
        in_specs=[smem, smem, vmem] + [vmem] * len(arrays),
        out_specs=(
            pl.BlockSpec((rows, GROUP * D), lambda i: (0, i)),
            pl.BlockSpec((GROUP, rows), lambda i: (i, 0)),
        ),
        scratch_shapes=[pltpu.VMEM((12 * T, D), jnp.bfloat16), pltpu.VMEM((12 * T, 2 * D), jnp.bfloat16)],
        compiler_params=pltpu.CompilerParams(vmem_limit_bytes=40 * 2**20),
        cost_estimate=pl.CostEstimate(flops=2_400_000_000, bytes_accessed=8_000_000, transcendentals=4_800_000),
        name="attention",
    )(meta, spans, q, *arrays)


def local(n_inner, n_outer, queries, keys, values, spans):
    n_high = n_inner // (Y * CORES)

    def at(high, y, core, o):
        return ((high % n_high * Y + y % Y) * CORES + core) * n_outer + o % n_outer

    def send(block, moves):
        route = [
            (at(*source, o), at(*target, o))
            for high in range(n_high)
            for o in range(n_outer)
            for source, target in moves(high)
        ]
        return lax.ppermute(block, AXES, sorted(route))

    inner_at = lax.axis_index("inner")
    outer_at = lax.axis_index("outer")
    meta = jnp.stack(
        [
            inner_at * n_outer + outer_at,
            (inner_at - 1) % n_inner * n_outer + outer_at,
            (inner_at - 2) % n_inner * n_outer + outer_at,
            inner_at * n_outer + (outer_at - 1) % n_outer,
            (inner_at % CORES == 0).astype(jnp.int32),
            (inner_at // CORES % Y == 0).astype(jnp.int32),
        ]
    ).astype(jnp.int32)
    first_spans = spans[:, 0]
    meta, first_spans = lax.optimization_barrier((meta, first_spans))

    last = Y - 1

    def send_outer(block):
        route = [
            (i * n_outer + o, i * n_outer + (o + 1) % n_outer)
            for i in range(n_inner)
            for o in range(n_outer)
        ]
        return lax.ppermute(block, AXES, route)

    rows, width = keys.shape
    cut = 2 * rows * 9 // 16
    both, relayed, straight = pack(values, keys, cut)
    spread = send(relayed, lambda h: [((h, last, 0), (h, 1, 0)), ((h, last, 1), (h, 2, 1))])
    straight = send(straight, lambda h: [((h, last, c), (h + 1, 0, c)) for c in range(CORES)])
    crossed = send(spread, lambda h: [((h, 1, 0), (h + 1, 0, 0)), ((h, 2, 1), (h + 1, 0, 1))])
    (crossed,) = small_kernel(join_body, "join", JOIN, [(2 * rows, width)], crossed, straight)
    both, spread = lax.optimization_barrier((both, spread))
    side = send_outer(both)
    stepped = send(both, lambda h: [((h, y, c), (h, y + 1, c)) for y in range(last) for c in range(CORES)])
    handed = send(both, lambda h: [((h, y, 0), (h, y, 1)) for y in range(Y)])
    (far,) = small_kernel(choose_body, "choose", 1_000, [(2 * rows, width)], meta, crossed, stepped)
    last_near = send(far, lambda h: [((h, y, 1), (h, y, 0)) for y in range(Y)])
    return attention(
        meta, first_spans, queries, (keys, 0), (values, 0), (handed, 1), (handed, 0), (last_near, 1), (last_near, 0),
        (far, 1), (far, 0), (side, 1), (side, 0),
    )


def solution(mesh):
    placed = P(AXES, None)
    return jax.shard_map(
        lambda *args: tuple(local(mesh.shape["inner"], mesh.shape["outer"], *args)),
        mesh=mesh,
        in_specs=(placed, placed, placed, P()),
        out_specs=(placed, P(None, AXES)),
        check_vma=False,
    )
```

```python
import functools
import math

import jax
import jax.numpy as jnp
from jax import lax
from jax.experimental import pallas as pl
from jax.experimental.pallas import tpu as pltpu
from jax.sharding import PartitionSpec as P

D = 128
T = 128
GROUP = 8
CHUNK = 4
LOG2E = math.log2(math.e)
SCALE = D**-0.5 * LOG2E
AXES = ("inner", "outer")
Y = 4
CORES = 2
JOIN = 20_000_000_000


def scores_of(q, k_ref, first, n):
    keys = k_ref[first * T : (first + n) * T, :]
    return lax.dot_general(q, keys, (((1,), (1,)), ((), ())), preferred_element_type=jnp.float32)


def weigh(scores, v_ref, first, n, masks):
    parts = [scores[:, i * T : (i + 1) * T] for i in range(n)]
    for i, mask in masks.items():
        parts[i] = jnp.where(mask, parts[i], -jnp.inf)
    top = jnp.max(functools.reduce(jnp.maximum, parts), axis=1, keepdims=True) * SCALE
    weights = jnp.concatenate([jnp.exp2(x * SCALE - top).astype(jnp.bfloat16) for x in parts], axis=1)
    values = v_ref[first * T : (first + n) * T, :]
    summed = lax.dot_general(weights, values, (((1,), (0,)), ((), ())), preferred_element_type=jnp.float32)
    return top, summed[:, :D], summed[:, D:]


def attention_body(
    meta, spans, q_ref, k_ref, v_ref, handed_k, handed_v, last_k, last_v,
    far_k, far_v, side_k, side_v, out_ref, log_ref, k_all, v_all,
):
    def place(i):
        a = spans[meta[i]]
        flip = a >= 512
        return jnp.where(flip, 1023 - a, a), jnp.where(flip, T, 0), jnp.where(flip, 0, T)

    def rows_at(start):
        return pl.ds(pl.multiple_of(start, T), T)

    at_even = meta[4] == 1

    def near(rows):
        return (
            jnp.where(at_even, last_k[rows, :], handed_k[rows, :]),
            jnp.where(at_even, last_v[rows, :], handed_v[rows, :]),
        )

    def far(rows):
        return far_k[rows, :], far_v[rows, :]

    def side(rows):
        return side_k[rows, :], side_v[rows, :]

    ones = jnp.ones((T, D), v_all.dtype)

    def put(slot, pair, weight=ones):
        rows = rows_at(slot * T)
        k_all[rows, :], v_all[rows, :D] = pair
        v_all[rows, D:] = weight

    own, low_at, high_at = place(0)
    ends = (rows_at(low_at), rows_at(high_at))
    own_low = (k_ref[ends[0], :], v_ref[ends[0], :])
    put(0, own_low)
    put(4, (k_ref[ends[1], :], v_ref[ends[1], :]))
    put(5, own_low)
    n_low = jnp.int32(0)
    for i, read in enumerate((near, far, side)):
        block, block_low, block_high = place(i + 1)
        below = block < own
        put(6 + i, read(rows_at(block_low)))
        put(jnp.where(below, 1 + n_low, 9 + i - n_low), read(rows_at(jnp.where(below, block_low, block_high))))
        n_low = n_low + below.astype(jnp.int32)
    many = n_low >= 2
    spare = jnp.where(many, jnp.where(n_low == 2, 3, 9), jnp.where(n_low == 0, 1, 11))
    none = jnp.zeros((T, D), v_all.dtype)
    put(spare, (jnp.where(n_low == 2, k_all[T : 2 * T, :], own_low[0]), none), none)

    row = lax.broadcasted_iota(jnp.int32, (CHUNK * T, T), 0) % T
    col = lax.broadcasted_iota(jnp.int32, (CHUNK * T, T), 1)
    lane = lax.broadcasted_iota(jnp.int32, (T, T), 1)
    cols = [slice(j * D, (j + 1) * D) for j in range(GROUP)]

    def all_heads(low_tiles):
        first, tiles = (0, 4), (low_tiles, 10 - low_tiles)
        masks = [{0: col <= row}, {0: col <= row}]
        if low_tiles == 2:
            masks[0][1] = col <= jnp.where(n_low == 0, row, T)
        tops, totals = [None, None], [None, None]

        def finish(w, g, scores):
            top, summed, total = weigh(scores, v_all, first[w], tiles[w], masks[w])
            result = (summed * pl.reciprocal(total)).astype(out_ref.dtype)
            for j in range(CHUNK):
                part = slice(j * T, (j + 1) * T)
                out_ref[ends[w], cols[g + j]] = result[part]
                for kept, new in ((tops, top[part]), (totals, total[part])):
                    new = jnp.broadcast_to(new, (T, T))
                    kept[w] = new if kept[w] is None else jnp.where(lane == g + j, new, kept[w])

        waiting = None
        for g in range(0, GROUP, CHUNK):
            for w in (0, 1):
                q = jnp.concatenate([q_ref[ends[w], cols[g + j]] for j in range(CHUNK)], axis=0)
                scores = scores_of(q, k_all, first[w], tiles[w])
                if waiting:
                    finish(*waiting)
                waiting = (w, g, scores)
        finish(*waiting)
        for w in (0, 1):
            log_sum = (tops[w] + jnp.log2(totals[w])) * (1.0 / LOG2E)
            log_ref[:, ends[w]] = jnp.transpose(log_sum)[:GROUP]

    for low_tiles in (2, 4):
        pl.when(many == (low_tiles == 4))(functools.partial(all_heads, low_tiles))


def small_kernel(body, name, flops, outs, *arrays):
    smem = pl.BlockSpec(memory_space=pltpu.SMEM)
    return pl.pallas_call(
        body,
        out_shape=[jax.ShapeDtypeStruct(shape, arrays[-1].dtype) for shape in outs],
        in_specs=[smem if a.ndim == 1 else pl.BlockSpec(a.shape, lambda: (0, 0)) for a in arrays],
        out_specs=[pl.BlockSpec(shape, lambda: (0, 0)) for shape in outs],
        compiler_params=pltpu.CompilerParams(vmem_limit_bytes=16 * 2**20),
        cost_estimate=pl.CostEstimate(flops=flops, bytes_accessed=1_000_000, transcendentals=0),
        name=name,
    )(*arrays)


def pack_body(upper, lower, both, sems):
    rows = upper.shape[0]
    copies = [
        pltpu.make_async_copy(upper, both.at[:rows], sems.at[0]),
        pltpu.make_async_copy(lower, both.at[rows:], sems.at[1]),
    ]
    for copy in copies:
        copy.start()
    for copy in copies:
        copy.wait()


def pack(upper, lower):
    rows, width = upper.shape
    return pl.pallas_call(
        pack_body,
        out_shape=jax.ShapeDtypeStruct((2 * rows, width), upper.dtype),
        in_specs=[pl.BlockSpec(memory_space=pl.ANY)] * 2,
        out_specs=pl.BlockSpec(memory_space=pltpu.VMEM),
        scratch_shapes=[pltpu.SemaphoreType.DMA((2,))],
        compiler_params=pltpu.CompilerParams(vmem_limit_bytes=56 * 2**20),
        name="pack",
    )(upper, lower)


def join_body(upper, lower, out):
    rows = upper.shape[0]
    out[:rows, :] = upper[...]
    out[rows:, :] = lower[...]


def choose_body(meta, first, second, out):
    @pl.when(meta[5] == 1)
    def _():
        out[...] = first[...]

    @pl.when(meta[5] == 0)
    def _():
        out[...] = second[...]


def attention(meta, spans, q, *blocks):
    rows, width = q.shape
    smem = pl.BlockSpec(memory_space=pltpu.SMEM)
    vmem = pl.BlockSpec(memory_space=pltpu.VMEM)
    arrays = list({id(array): array for array, _ in blocks}.values())
    where = [([id(a) for a in arrays].index(id(array)), at) for array, at in blocks]

    def body(meta_ref, spans_ref, q_ref, *refs):
        kv = pl.program_id(0)
        columns = pl.ds(pl.multiple_of(kv * D, D), D)
        views = [refs[i].at[at * rows : (at + 1) * rows, columns] for i, at in where]
        q_view = q_ref.at[:, pl.ds(pl.multiple_of(kv * GROUP * D, D), GROUP * D)]
        attention_body(meta_ref, spans_ref, q_view, *views, *refs[len(arrays) :])

    return pl.pallas_call(
        body,
        grid=(width // (GROUP * D),),
        out_shape=(
            jax.ShapeDtypeStruct((rows, width), jnp.bfloat16),
            jax.ShapeDtypeStruct((width // D, rows), jnp.float32),
        ),
        in_specs=[smem, smem, vmem] + [vmem] * len(arrays),
        out_specs=(
            pl.BlockSpec((rows, GROUP * D), lambda i: (0, i)),
            pl.BlockSpec((GROUP, rows), lambda i: (i, 0)),
        ),
        scratch_shapes=[pltpu.VMEM((12 * T, D), jnp.bfloat16), pltpu.VMEM((12 * T, 2 * D), jnp.bfloat16)],
        compiler_params=pltpu.CompilerParams(vmem_limit_bytes=40 * 2**20),
        cost_estimate=pl.CostEstimate(flops=2_400_000_000, bytes_accessed=8_000_000, transcendentals=4_800_000),
        name="attention",
    )(meta, spans, q, *arrays)


def local(n_inner, n_outer, queries, keys, values, spans):
    n_high = n_inner // (Y * CORES)

    def at(high, y, core, o):
        return ((high % n_high * Y + y % Y) * CORES + core) * n_outer + o % n_outer

    def send(block, moves):
        route = [
            (at(*source, o), at(*target, o))
            for high in range(n_high)
            for o in range(n_outer)
            for source, target in moves(high)
        ]
        return lax.ppermute(block, AXES, sorted(route))

    inner_at = lax.axis_index("inner")
    outer_at = lax.axis_index("outer")
    meta = jnp.stack(
        [
            inner_at * n_outer + outer_at,
            (inner_at - 1) % n_inner * n_outer + outer_at,
            (inner_at - 2) % n_inner * n_outer + outer_at,
            inner_at * n_outer + (outer_at - 1) % n_outer,
            (inner_at % CORES == 0).astype(jnp.int32),
            (inner_at // CORES % Y == 0).astype(jnp.int32),
        ]
    ).astype(jnp.int32)
    first_spans = spans[:, 0]
    meta, first_spans = lax.optimization_barrier((meta, first_spans))

    last = Y - 1

    def send_outer(block):
        route = [
            (i * n_outer + o, i * n_outer + (o + 1) % n_outer)
            for i in range(n_inner)
            for o in range(n_outer)
        ]
        return lax.ppermute(block, AXES, route)

    rows, width = keys.shape
    spread = send(values, lambda h: [((h, last, 0), (h, 1, 0)), ((h, last, 1), (h, 2, 1))])
    straight = send(keys, lambda h: [((h, last, c), (h + 1, 0, c)) for c in range(CORES)])
    crossed = send(spread, lambda h: [((h, 1, 0), (h + 1, 0, 0)), ((h, 2, 1), (h + 1, 0, 1))])
    (crossed,) = small_kernel(join_body, "join", JOIN, [(2 * rows, width)], crossed, straight)
    late_k, late_v, spread = lax.optimization_barrier((keys, values, spread))
    both = pack(late_v, late_k)
    side = send_outer(both)
    stepped = send(both, lambda h: [((h, y, c), (h, y + 1, c)) for y in range(last) for c in range(CORES)])
    handed = send(both, lambda h: [((h, y, 0), (h, y, 1)) for y in range(Y)])
    (far,) = small_kernel(choose_body, "choose", 1_000, [(2 * rows, width)], meta, crossed, stepped)
    last_near = send(far, lambda h: [((h, y, 1), (h, y, 0)) for y in range(Y)])
    return attention(
        meta, first_spans, queries, (keys, 0), (values, 0), (handed, 1), (handed, 0), (last_near, 1), (last_near, 0),
        (far, 1), (far, 0), (side, 1), (side, 0),
    )


def solution(mesh):
    placed = P(AXES, None)
    return jax.shard_map(
        lambda *args: tuple(local(mesh.shape["inner"], mesh.shape["outer"], *args)),
        mesh=mesh,
        in_specs=(placed, placed, placed, P()),
        out_specs=(placed, P(None, AXES)),
        check_vma=False,
    )
```

```python
import functools
import math

import jax
import jax.numpy as jnp
from jax import lax
from jax.experimental import pallas as pl
from jax.experimental.pallas import tpu as pltpu
from jax.sharding import PartitionSpec as P

D = 128
T = 128
GROUP = 8
CHUNK = 4
LOG2E = math.log2(math.e)
SCALE = D**-0.5 * LOG2E
AXES = ("inner", "outer")
Y = 4
CORES = 2
JOIN = 20_000_000_000


def scores_of(q, k_ref, first, n):
    keys = k_ref[first * T : (first + n) * T, :]
    return lax.dot_general(q, keys, (((1,), (1,)), ((), ())), preferred_element_type=jnp.float32)


def weigh(scores, v_ref, first, n, masks):
    parts = [scores[:, i * T : (i + 1) * T] for i in range(n)]
    for i, mask in masks.items():
        parts[i] = jnp.where(mask, parts[i], -jnp.inf)
    top = jnp.max(functools.reduce(jnp.maximum, parts), axis=1, keepdims=True) * SCALE
    weights = jnp.concatenate([jnp.exp2(x * SCALE - top).astype(jnp.bfloat16) for x in parts], axis=1)
    values = v_ref[first * T : (first + n) * T, :]
    summed = lax.dot_general(weights, values, (((1,), (0,)), ((), ())), preferred_element_type=jnp.float32)
    return top, summed[:, :D], summed[:, D:]


def attention_body(
    meta, spans, q_ref, k_ref, v_ref, handed_k, handed_v, last_k, last_v,
    far_k, far_v, side_k, side_v, out_ref, log_ref, k_all, v_all,
):
    def place(i):
        a = spans[meta[i]]
        flip = a >= 512
        return jnp.where(flip, 1023 - a, a), jnp.where(flip, T, 0), jnp.where(flip, 0, T)

    def rows_at(start):
        return pl.ds(pl.multiple_of(start, T), T)

    at_even = meta[4] == 1

    def near(rows):
        return (
            jnp.where(at_even, last_k[rows, :], handed_k[rows, :]),
            jnp.where(at_even, last_v[rows, :], handed_v[rows, :]),
        )

    def far(rows):
        return far_k[rows, :], far_v[rows, :]

    def side(rows):
        return side_k[rows, :], side_v[rows, :]

    ones = jnp.ones((T, D), v_all.dtype)

    def put(slot, pair, weight=ones):
        rows = rows_at(slot * T)
        k_all[rows, :], v_all[rows, :D] = pair
        v_all[rows, D:] = weight

    own, low_at, high_at = place(0)
    ends = (rows_at(low_at), rows_at(high_at))
    own_low = (k_ref[ends[0], :], v_ref[ends[0], :])
    put(0, own_low)
    put(4, (k_ref[ends[1], :], v_ref[ends[1], :]))
    put(5, own_low)
    n_low = jnp.int32(0)
    for i, read in enumerate((near, far, side)):
        block, block_low, block_high = place(i + 1)
        below = block < own
        put(6 + i, read(rows_at(block_low)))
        put(jnp.where(below, 1 + n_low, 9 + i - n_low), read(rows_at(jnp.where(below, block_low, block_high))))
        n_low = n_low + below.astype(jnp.int32)
    many = n_low >= 2
    spare = jnp.where(many, jnp.where(n_low == 2, 3, 9), jnp.where(n_low == 0, 1, 11))
    none = jnp.zeros((T, D), v_all.dtype)
    put(spare, (jnp.where(n_low == 2, k_all[T : 2 * T, :], own_low[0]), none), none)

    row = lax.broadcasted_iota(jnp.int32, (CHUNK * T, T), 0) % T
    col = lax.broadcasted_iota(jnp.int32, (CHUNK * T, T), 1)
    lane = lax.broadcasted_iota(jnp.int32, (T, T), 1)
    cols = [slice(j * D, (j + 1) * D) for j in range(GROUP)]

    def all_heads(low_tiles):
        first, tiles = (0, 4), (low_tiles, 10 - low_tiles)
        masks = [{0: col <= row}, {0: col <= row}]
        if low_tiles == 2:
            masks[0][1] = col <= jnp.where(n_low == 0, row, T)
        tops, totals = [None, None], [None, None]

        def finish(w, g, scores):
            top, summed, total = weigh(scores, v_all, first[w], tiles[w], masks[w])
            result = (summed * pl.reciprocal(total)).astype(out_ref.dtype)
            for j in range(CHUNK):
                part = slice(j * T, (j + 1) * T)
                out_ref[ends[w], cols[g + j]] = result[part]
                for kept, new in ((tops, top[part]), (totals, total[part])):
                    new = jnp.broadcast_to(new, (T, T))
                    kept[w] = new if kept[w] is None else jnp.where(lane == g + j, new, kept[w])

        waiting = None
        for g in range(0, GROUP, CHUNK):
            for w in (0, 1):
                q = jnp.concatenate([q_ref[ends[w], cols[g + j]] for j in range(CHUNK)], axis=0)
                scores = scores_of(q, k_all, first[w], tiles[w])
                if waiting:
                    finish(*waiting)
                waiting = (w, g, scores)
        finish(*waiting)
        for w in (0, 1):
            log_sum = (tops[w] + jnp.log2(totals[w])) * (1.0 / LOG2E)
            log_ref[:, ends[w]] = jnp.transpose(log_sum)[:GROUP]

    for low_tiles in (2, 4):
        pl.when(many == (low_tiles == 4))(functools.partial(all_heads, low_tiles))


def small_kernel(body, name, flops, outs, *arrays):
    smem = pl.BlockSpec(memory_space=pltpu.SMEM)
    return pl.pallas_call(
        body,
        out_shape=[jax.ShapeDtypeStruct(shape, arrays[-1].dtype) for shape in outs],
        in_specs=[smem if a.ndim == 1 else pl.BlockSpec(a.shape, lambda: (0, 0)) for a in arrays],
        out_specs=[pl.BlockSpec(shape, lambda: (0, 0)) for shape in outs],
        compiler_params=pltpu.CompilerParams(vmem_limit_bytes=16 * 2**20),
        cost_estimate=pl.CostEstimate(flops=flops, bytes_accessed=1_000_000, transcendentals=0),
        name=name,
    )(*arrays)


def pack_body(upper, lower, both, sems):
    rows = upper.shape[0]
    copies = [
        pltpu.make_async_copy(upper, both.at[:rows], sems.at[0]),
        pltpu.make_async_copy(lower, both.at[rows:], sems.at[1]),
    ]
    for copy in copies:
        copy.start()
    for copy in copies:
        copy.wait()


def pack(upper, lower):
    rows, width = upper.shape
    return pl.pallas_call(
        pack_body,
        out_shape=jax.ShapeDtypeStruct((2 * rows, width), upper.dtype),
        in_specs=[pl.BlockSpec(memory_space=pl.ANY)] * 2,
        out_specs=pl.BlockSpec(memory_space=pltpu.VMEM),
        scratch_shapes=[pltpu.SemaphoreType.DMA((2,))],
        compiler_params=pltpu.CompilerParams(vmem_limit_bytes=56 * 2**20),
        name="pack",
    )(upper, lower)


def join_body(upper, middle, lower, out):
    rows, half = upper.shape[0], middle.shape[0]
    out[:rows, :] = upper[...]
    out[rows : rows + half, :] = middle[...]
    out[rows + half :, :] = lower[...]


def choose_body(meta, first, second, out):
    @pl.when(meta[5] == 1)
    def _():
        out[...] = first[...]

    @pl.when(meta[5] == 0)
    def _():
        out[...] = second[...]


def attention(meta, spans, q, *blocks):
    rows, width = q.shape
    smem = pl.BlockSpec(memory_space=pltpu.SMEM)
    vmem = pl.BlockSpec(memory_space=pltpu.VMEM)
    arrays = list({id(array): array for array, _ in blocks}.values())
    where = [([id(a) for a in arrays].index(id(array)), at) for array, at in blocks]

    def body(meta_ref, spans_ref, q_ref, *refs):
        kv = pl.program_id(0)
        columns = pl.ds(pl.multiple_of(kv * D, D), D)
        views = [refs[i].at[at * rows : (at + 1) * rows, columns] for i, at in where]
        q_view = q_ref.at[:, pl.ds(pl.multiple_of(kv * GROUP * D, D), GROUP * D)]
        attention_body(meta_ref, spans_ref, q_view, *views, *refs[len(arrays) :])

    return pl.pallas_call(
        body,
        grid=(width // (GROUP * D),),
        out_shape=(
            jax.ShapeDtypeStruct((rows, width), jnp.bfloat16),
            jax.ShapeDtypeStruct((width // D, rows), jnp.float32),
        ),
        in_specs=[smem, smem, vmem] + [vmem] * len(arrays),
        out_specs=(
            pl.BlockSpec((rows, GROUP * D), lambda i: (0, i)),
            pl.BlockSpec((GROUP, rows), lambda i: (i, 0)),
        ),
        scratch_shapes=[pltpu.VMEM((12 * T, D), jnp.bfloat16), pltpu.VMEM((12 * T, 2 * D), jnp.bfloat16)],
        compiler_params=pltpu.CompilerParams(vmem_limit_bytes=40 * 2**20),
        cost_estimate=pl.CostEstimate(flops=2_400_000_000, bytes_accessed=8_000_000, transcendentals=4_800_000),
        name="attention",
    )(meta, spans, q, *arrays)


def local(n_inner, n_outer, queries, keys, values, spans):
    n_high = n_inner // (Y * CORES)

    def at(high, y, core, o):
        return ((high % n_high * Y + y % Y) * CORES + core) * n_outer + o % n_outer

    def send(block, moves):
        route = [
            (at(*source, o), at(*target, o))
            for high in range(n_high)
            for o in range(n_outer)
            for source, target in moves(high)
        ]
        return lax.ppermute(block, AXES, sorted(route))

    inner_at = lax.axis_index("inner")
    outer_at = lax.axis_index("outer")
    meta = jnp.stack(
        [
            inner_at * n_outer + outer_at,
            (inner_at - 1) % n_inner * n_outer + outer_at,
            (inner_at - 2) % n_inner * n_outer + outer_at,
            inner_at * n_outer + (outer_at - 1) % n_outer,
            (inner_at % CORES == 0).astype(jnp.int32),
            (inner_at // CORES % Y == 0).astype(jnp.int32),
        ]
    ).astype(jnp.int32)
    first_spans = spans[:, 0]
    meta, first_spans = lax.optimization_barrier((meta, first_spans))

    last = Y - 1

    def send_outer(block):
        route = [
            (i * n_outer + o, i * n_outer + (o + 1) % n_outer)
            for i in range(n_inner)
            for o in range(n_outer)
        ]
        return lax.ppermute(block, AXES, route)

    rows, width = keys.shape
    spread = send(values, lambda h: [((h, last, 0), (h, 1, 0)), ((h, last, 1), (h, 2, 1))])
    straight = send(keys[: rows // 2], lambda h: [((h, last, c), (h + 1, 0, c)) for c in range(CORES)])
    spread_k = send(keys[rows // 2 :], lambda h: [((h, last, c), (h, 0, c)) for c in range(CORES)])
    turned = send(spread_k, lambda h: [((h, 0, c), (h + 1, 0, c)) for c in range(CORES)])
    crossed = send(spread, lambda h: [((h, 1, 0), (h + 1, 0, 0)), ((h, 2, 1), (h + 1, 0, 1))])
    (crossed,) = small_kernel(join_body, "join", JOIN, [(2 * rows, width)], crossed, straight, turned)
    late_k, late_v, spread = lax.optimization_barrier((keys, values, spread))
    both = pack(late_v, late_k)
    side = send_outer(both)
    stepped = send(both, lambda h: [((h, y, c), (h, y + 1, c)) for y in range(last) for c in range(CORES)])
    handed = send(both, lambda h: [((h, y, 0), (h, y, 1)) for y in range(Y)])
    (far,) = small_kernel(choose_body, "choose", 1_000, [(2 * rows, width)], meta, crossed, stepped)
    last_near = send(far, lambda h: [((h, y, 1), (h, y, 0)) for y in range(Y)])
    return attention(
        meta, first_spans, queries, (keys, 0), (values, 0), (handed, 1), (handed, 0), (last_near, 1), (last_near, 0),
        (far, 1), (far, 0), (side, 1), (side, 0),
    )


def solution(mesh):
    placed = P(AXES, None)
    return jax.shard_map(
        lambda *args: tuple(local(mesh.shape["inner"], mesh.shape["outer"], *args)),
        mesh=mesh,
        in_specs=(placed, placed, placed, P()),
        out_specs=(placed, P(None, AXES)),
        check_vma=False,
    )
```

```python
import functools
import math

import jax
import jax.numpy as jnp
from jax import lax
from jax.experimental import pallas as pl
from jax.experimental.pallas import tpu as pltpu
from jax.sharding import PartitionSpec as P

D = 128
T = 128
GROUP = 8
CHUNK = 4
LOG2E = math.log2(math.e)
SCALE = D**-0.5 * LOG2E
AXES = ("inner", "outer")
Y = 4
CORES = 2
JOIN = 20_000_000_000


def scores_of(q, k_ref, first, n):
    keys = k_ref[first * T : (first + n) * T, :]
    return lax.dot_general(q, keys, (((1,), (1,)), ((), ())), preferred_element_type=jnp.float32)


def weigh(scores, v_ref, first, n, masks):
    parts = [scores[:, i * T : (i + 1) * T] for i in range(n)]
    for i, mask in masks.items():
        parts[i] = jnp.where(mask, parts[i], -jnp.inf)
    top = jnp.max(functools.reduce(jnp.maximum, parts), axis=1, keepdims=True) * SCALE
    weights = jnp.concatenate([jnp.exp2(x * SCALE - top).astype(jnp.bfloat16) for x in parts], axis=1)
    values = v_ref[first * T : (first + n) * T, :]
    summed = lax.dot_general(weights, values, (((1,), (0,)), ((), ())), preferred_element_type=jnp.float32)
    return top, summed[:, :D], summed[:, D:]


def attention_body(
    meta, spans, q_ref, k_ref, v_ref, handed_k, handed_v, last_k, last_v,
    far_k, far_v, side_k, side_v, out_ref, log_ref, k_all, v_all,
):
    def place(i):
        a = spans[meta[i]]
        flip = a >= 512
        return jnp.where(flip, 1023 - a, a), jnp.where(flip, T, 0), jnp.where(flip, 0, T)

    def rows_at(start):
        return pl.ds(pl.multiple_of(start, T), T)

    at_even = meta[4] == 1

    def near(rows):
        return (
            jnp.where(at_even, last_k[rows, :], handed_k[rows, :]),
            jnp.where(at_even, last_v[rows, :], handed_v[rows, :]),
        )

    def far(rows):
        return far_k[rows, :], far_v[rows, :]

    def side(rows):
        return side_k[rows, :], side_v[rows, :]

    ones = jnp.ones((T, D), v_all.dtype)

    def put(slot, pair, weight=ones):
        rows = rows_at(slot * T)
        k_all[rows, :], v_all[rows, :D] = pair
        v_all[rows, D:] = weight

    own, low_at, high_at = place(0)
    ends = (rows_at(low_at), rows_at(high_at))
    own_low = (k_ref[ends[0], :], v_ref[ends[0], :])
    put(0, own_low)
    put(4, (k_ref[ends[1], :], v_ref[ends[1], :]))
    put(5, own_low)
    n_low = jnp.int32(0)
    for i, read in enumerate((near, far, side)):
        block, block_low, block_high = place(i + 1)
        below = block < own
        put(6 + i, read(rows_at(block_low)))
        put(jnp.where(below, 1 + n_low, 9 + i - n_low), read(rows_at(jnp.where(below, block_low, block_high))))
        n_low = n_low + below.astype(jnp.int32)
    many = n_low >= 2
    spare = jnp.where(many, jnp.where(n_low == 2, 3, 9), jnp.where(n_low == 0, 1, 11))
    none = jnp.zeros((T, D), v_all.dtype)
    put(spare, (jnp.where(n_low == 2, k_all[T : 2 * T, :], own_low[0]), none), none)

    row = lax.broadcasted_iota(jnp.int32, (CHUNK * T, T), 0) % T
    col = lax.broadcasted_iota(jnp.int32, (CHUNK * T, T), 1)
    lane = lax.broadcasted_iota(jnp.int32, (T, T), 1)
    cols = [slice(j * D, (j + 1) * D) for j in range(GROUP)]

    def all_heads(low_tiles):
        first, tiles = (0, 4), (low_tiles, 10 - low_tiles)
        masks = [{0: col <= row}, {0: col <= row}]
        if low_tiles == 2:
            masks[0][1] = col <= jnp.where(n_low == 0, row, T)
        tops, totals = [None, None], [None, None]

        def finish(w, g, scores):
            top, summed, total = weigh(scores, v_all, first[w], tiles[w], masks[w])
            result = (summed * pl.reciprocal(total)).astype(out_ref.dtype)
            for j in range(CHUNK):
                part = slice(j * T, (j + 1) * T)
                out_ref[ends[w], cols[g + j]] = result[part]
                for kept, new in ((tops, top[part]), (totals, total[part])):
                    new = jnp.broadcast_to(new, (T, T))
                    kept[w] = new if kept[w] is None else jnp.where(lane == g + j, new, kept[w])

        waiting = None
        for g in range(0, GROUP, CHUNK):
            for w in (0, 1):
                q = jnp.concatenate([q_ref[ends[w], cols[g + j]] for j in range(CHUNK)], axis=0)
                scores = scores_of(q, k_all, first[w], tiles[w])
                if waiting:
                    finish(*waiting)
                waiting = (w, g, scores)
        finish(*waiting)
        for w in (0, 1):
            log_sum = (tops[w] + jnp.log2(totals[w])) * (1.0 / LOG2E)
            log_ref[:, ends[w]] = jnp.transpose(log_sum)[:GROUP]

    for low_tiles in (2, 4):
        pl.when(many == (low_tiles == 4))(functools.partial(all_heads, low_tiles))


def small_kernel(body, name, flops, outs, *arrays):
    smem = pl.BlockSpec(memory_space=pltpu.SMEM)
    return pl.pallas_call(
        body,
        out_shape=[jax.ShapeDtypeStruct(shape, arrays[-1].dtype) for shape in outs],
        in_specs=[smem if a.ndim == 1 else pl.BlockSpec(a.shape, lambda: (0, 0)) for a in arrays],
        out_specs=[pl.BlockSpec(shape, lambda: (0, 0)) for shape in outs],
        compiler_params=pltpu.CompilerParams(vmem_limit_bytes=16 * 2**20),
        cost_estimate=pl.CostEstimate(flops=flops, bytes_accessed=1_000_000, transcendentals=0),
        name=name,
    )(*arrays)


def pack_body(upper, lower, both, sems):
    rows = upper.shape[0]
    copies = [
        pltpu.make_async_copy(upper, both.at[:rows], sems.at[0]),
        pltpu.make_async_copy(lower, both.at[rows:], sems.at[1]),
    ]
    for copy in copies:
        copy.start()
    for copy in copies:
        copy.wait()


def pack(upper, lower):
    rows, width = upper.shape
    return pl.pallas_call(
        pack_body,
        out_shape=jax.ShapeDtypeStruct((2 * rows, width), upper.dtype),
        in_specs=[pl.BlockSpec(memory_space=pl.ANY)] * 2,
        out_specs=pl.BlockSpec(memory_space=pltpu.VMEM),
        scratch_shapes=[pltpu.SemaphoreType.DMA((2,))],
        compiler_params=pltpu.CompilerParams(vmem_limit_bytes=56 * 2**20),
        name="pack",
    )(upper, lower)


def join_body(upper, middle, lower, out):
    rows, cut = out.shape[0] // 2, upper.shape[0]
    half = rows // 2
    more = middle.shape[0] - half
    out[:cut, :] = upper[...]
    out[cut : cut + more, :] = middle[half:, :]
    out[cut + more : rows, :] = lower[half:, :]
    out[rows : rows + half, :] = middle[:half, :]
    out[rows + half :, :] = lower[:half, :]


def choose_body(meta, first, second, out):
    @pl.when(meta[5] == 1)
    def _():
        out[...] = first[...]

    @pl.when(meta[5] == 0)
    def _():
        out[...] = second[...]


def attention(meta, spans, q, *blocks):
    rows, width = q.shape
    smem = pl.BlockSpec(memory_space=pltpu.SMEM)
    vmem = pl.BlockSpec(memory_space=pltpu.VMEM)
    arrays = list({id(array): array for array, _ in blocks}.values())
    where = [([id(a) for a in arrays].index(id(array)), at) for array, at in blocks]

    def body(meta_ref, spans_ref, q_ref, *refs):
        kv = pl.program_id(0)
        columns = pl.ds(pl.multiple_of(kv * D, D), D)
        views = [refs[i].at[at * rows : (at + 1) * rows, columns] for i, at in where]
        q_view = q_ref.at[:, pl.ds(pl.multiple_of(kv * GROUP * D, D), GROUP * D)]
        attention_body(meta_ref, spans_ref, q_view, *views, *refs[len(arrays) :])

    return pl.pallas_call(
        body,
        grid=(width // (GROUP * D),),
        out_shape=(
            jax.ShapeDtypeStruct((rows, width), jnp.bfloat16),
            jax.ShapeDtypeStruct((width // D, rows), jnp.float32),
        ),
        in_specs=[smem, smem, vmem] + [vmem] * len(arrays),
        out_specs=(
            pl.BlockSpec((rows, GROUP * D), lambda i: (0, i)),
            pl.BlockSpec((GROUP, rows), lambda i: (i, 0)),
        ),
        scratch_shapes=[pltpu.VMEM((12 * T, D), jnp.bfloat16), pltpu.VMEM((12 * T, 2 * D), jnp.bfloat16)],
        compiler_params=pltpu.CompilerParams(vmem_limit_bytes=40 * 2**20),
        cost_estimate=pl.CostEstimate(flops=2_400_000_000, bytes_accessed=8_000_000, transcendentals=4_800_000),
        name="attention",
    )(meta, spans, q, *arrays)


def local(n_inner, n_outer, queries, keys, values, spans):
    n_high = n_inner // (Y * CORES)

    def at(high, y, core, o):
        return ((high % n_high * Y + y % Y) * CORES + core) * n_outer + o % n_outer

    def send(block, moves):
        route = [
            (at(*source, o), at(*target, o))
            for high in range(n_high)
            for o in range(n_outer)
            for source, target in moves(high)
        ]
        return lax.ppermute(block, AXES, sorted(route))

    inner_at = lax.axis_index("inner")
    outer_at = lax.axis_index("outer")
    meta = jnp.stack(
        [
            inner_at * n_outer + outer_at,
            (inner_at - 1) % n_inner * n_outer + outer_at,
            (inner_at - 2) % n_inner * n_outer + outer_at,
            inner_at * n_outer + (outer_at - 1) % n_outer,
            (inner_at % CORES == 0).astype(jnp.int32),
            (inner_at // CORES % Y == 0).astype(jnp.int32),
        ]
    ).astype(jnp.int32)
    first_spans = spans[:, 0]
    meta, first_spans = lax.optimization_barrier((meta, first_spans))

    last = Y - 1

    def send_outer(block):
        route = [
            (i * n_outer + o, i * n_outer + (o + 1) % n_outer)
            for i in range(n_inner)
            for o in range(n_outer)
        ]
        return lax.ppermute(block, AXES, route)

    rows, width = keys.shape
    half, cut = rows // 2, rows * 3 // 4
    middle = (cut + rows) // 2
    spread = send(values[:cut], lambda h: [((h, last, 0), (h, 1, 0)), ((h, last, 1), (h, 2, 1))])
    straight = jnp.concatenate([keys[:half], values[cut:middle]], axis=0)
    straight = send(straight, lambda h: [((h, last, c), (h + 1, 0, c)) for c in range(CORES)])
    spread_k = jnp.concatenate([keys[half:], values[middle:]], axis=0)
    spread_k = send(spread_k, lambda h: [((h, last, c), (h, 0, c)) for c in range(CORES)])
    turned = send(spread_k, lambda h: [((h, 0, c), (h + 1, 0, c)) for c in range(CORES)])
    crossed = send(spread, lambda h: [((h, 1, 0), (h + 1, 0, 0)), ((h, 2, 1), (h + 1, 0, 1))])
    (crossed,) = small_kernel(join_body, "join", JOIN, [(2 * rows, width)], crossed, straight, turned)
    late_k, late_v, spread = lax.optimization_barrier((keys, values, spread))
    both = pack(late_v, late_k)
    side = send_outer(both)
    stepped = send(both, lambda h: [((h, y, c), (h, y + 1, c)) for y in range(last) for c in range(CORES)])
    handed = send(both, lambda h: [((h, y, 0), (h, y, 1)) for y in range(Y)])
    (far,) = small_kernel(choose_body, "choose", 1_000, [(2 * rows, width)], meta, crossed, stepped)
    last_near = send(far, lambda h: [((h, y, 1), (h, y, 0)) for y in range(Y)])
    return attention(
        meta, first_spans, queries, (keys, 0), (values, 0), (handed, 1), (handed, 0), (last_near, 1), (last_near, 0),
        (far, 1), (far, 0), (side, 1), (side, 0),
    )


def solution(mesh):
    placed = P(AXES, None)
    return jax.shard_map(
        lambda *args: tuple(local(mesh.shape["inner"], mesh.shape["outer"], *args)),
        mesh=mesh,
        in_specs=(placed, placed, placed, P()),
        out_specs=(placed, P(None, AXES)),
        check_vma=False,
    )
```
